512 devices in a mesh: tm: 128 (over z_lo, x, y, core), series: 4 (over z_hi).
Axes of the slice: x: 4, y: 8, z: 8 (z_hi: 4, z_lo: 2; z = z_hi * 2 + z_lo), core: 2. Of those that a mesh axis runs over, the one named last changes fastest.
Arguments:
- time_query: bfloat16 [20, 8192, 512], P('series', 'tm'), may hold values from -160 to 160
- time_key: bfloat16 [20, 8192, 512], P('series', 'tm'), may hold values from -6 to 6
- time_value: bfloat16 [20, 8192, 512], P('series', 'tm'), may hold values from -6 to 6
- group_query: bfloat16 [20, 8192, 512], P('series', 'tm'), may hold values from -160 to 160
- group_key: bfloat16 [20, 8192, 512], P('series', 'tm'), may hold values from -6 to 6
- group_value: bfloat16 [20, 8192, 512], P('series', 'tm'), may hold values from -6 to 6
- out_time: bfloat16 [512, 768], P('series'), may hold values from -0.25 to 0.25
- out_group: bfloat16 [512, 768], P('series'), may hold values from -0.25 to 0.25
- series_group: int32 [20], replicated, may hold values from 0 to 1, as said below
- band_width: int32 [8], replicated, may hold values from 2 to 16, as said below
- cotangent: bfloat16 [20, 8192, 768], P('series', 'tm'), may hold values from -6 to 6
Outputs:
- grad_time_query: bfloat16 [20, 8192, 512], P('series', 'tm')
- grad_time_key: bfloat16 [20, 8192, 512], P('series', 'tm')
- grad_time_value: bfloat16 [20, 8192, 512], P('series', 'tm')
- grad_group_query: bfloat16 [20, 8192, 512], P('series', 'tm')
- grad_group_key: bfloat16 [20, 8192, 512], P('series', 'tm')
- grad_group_value: bfloat16 [20, 8192, 512], P('series', 'tm')
- grad_out_time: float32 [512, 768], P('series', 'tm')
- grad_out_group: float32 [512, 768], P('series', 'tm')
The draws below stay inside these ranges and needn't reach their ends.
Inputs may be any that keep to these rules, and one draw needn't show every extreme that they name: `series_group`: series with equal numbers form one group; there are two groups, one of exactly 16 series and one of exactly 4. `band_width`: some head's band is exactly 16.
All inputs are finite; a program needn't handle non-finite values.
Results may differ from the reference program's by a relative error of at most 0.0058.
Values may be sent and summed in bfloat16 or wider, within the bound.
No kernel may reach another device: no remote copies, remote signals or barrier semaphores. Data moves between devices by JAX's collectives and lax.ppermute only.
A program may use at most 128 MiB of HBM per device.

```python
import jax
import jax.numpy as jnp
from jax import lax

D = 768
HEADS = 8
HEAD_DIM = 64
BAND = 16
SERIES = 20
TIME = 8192
N_TM = 128


def shared_raw(key, salt):
    key = jax.random.fold_in(key, salt)
    first_key = jax.random.fold_in(key, 0)
    raw = jnp.clip(jax.random.normal(first_key, (SERIES, TIME, HEADS * HEAD_DIM), jnp.float32), -6.0, 6.0)
    return raw


def own_normal(key):
    return jnp.clip(jax.random.normal(key, (SERIES, TIME, HEADS * HEAD_DIM), jnp.float32), -6.0, 6.0)


def draw_time_key(key, part):
    raw = shared_raw(key, 101)
    return raw.astype(jnp.bfloat16)


def draw_time_query(key, part):
    key = jax.random.fold_in(key, 2)
    own = own_normal(key)
    return own.astype(jnp.bfloat16)


def draw_group_key(key, part):
    raw = shared_raw(key, 202)
    return raw.astype(jnp.bfloat16)


def draw_group_query(key, part):
    key = jax.random.fold_in(key, 4)
    own = own_normal(key)
    return own.astype(jnp.bfloat16)


def draw_series_group(key, part):
    key = jax.random.fold_in(key, 11)
    series_order = jax.random.permutation(key, SERIES)
    group_ids = (jnp.arange(SERIES) >= 16).astype(jnp.int32)
    return jnp.zeros((SERIES,), jnp.int32).at[series_order].set(group_ids)


def draw_band_width(key, part):
    key = jax.random.fold_in(key, 13)
    first_key, second_key = jax.random.split(key)
    widths = jax.random.randint(first_key, (HEADS,), 2, BAND + 1)
    chosen = jax.random.randint(second_key, (), 0, HEADS)
    return jnp.where(jnp.arange(HEADS) == chosen, BAND, widths).astype(jnp.int32)


def levels(own_key, shape, shards, low, largest):
    gain, own = 1.0, jax.random.fold_in(own_key, 6)
    for dim, parts in shards:
        heights = jnp.exp(jax.random.uniform(jax.random.fold_in(own, dim), (parts,), jnp.float32, low / len(shards), largest / len(shards)))
        gain = gain * jnp.repeat(heights, shape[dim] // parts).reshape([-1 if axis == dim else 1 for axis in range(len(shape))])
    return gain


def gaussian(rng, extent, spread, bound, pieces=(), held_as=jnp.bfloat16):
    loudness = levels(rng, extent, pieces, -0.22, 0.18) if pieces else 1.0
    values = jax.random.normal(rng, extent, jnp.float32) * spread * loudness
    return jnp.minimum(jnp.maximum(values, -bound), bound).astype(held_as)


def setup_inputs(seed: int = 0) -> dict:
    key_list = jax.random.split(jax.random.key(seed), 12)
    return {
        "time_query": draw_time_query(jax.random.fold_in(key_list[11], 71), 0),
        "time_key": draw_time_key(jax.random.fold_in(key_list[11], 71), 0),
        "time_value": gaussian(key_list[2], (SERIES, TIME, HEADS * HEAD_DIM), 1.0, 6.0, ((0, 4), (1, 128))),
        "group_query": draw_group_query(jax.random.fold_in(key_list[11], 71), 0),
        "group_key": draw_group_key(jax.random.fold_in(key_list[11], 71), 0),
        "group_value": gaussian(key_list[5], (SERIES, TIME, HEADS * HEAD_DIM), 1.0, 6.0, ((0, 4), (1, 128))),
        "out_time": gaussian(key_list[6], (HEADS * HEAD_DIM, D), (HEADS * HEAD_DIM) ** -0.5, 0.25, ((0, 4),)),
        "out_group": gaussian(key_list[7], (HEADS * HEAD_DIM, D), (HEADS * HEAD_DIM) ** -0.5, 0.25, ((0, 4),)),
        "series_group": draw_series_group(jax.random.fold_in(key_list[11], 71), 0),
        "band_width": draw_band_width(jax.random.fold_in(key_list[11], 71), 0),
        "cotangent": gaussian(key_list[10], (SERIES, TIME, D), 1.0, 6.0, ((0, 4), (1, 128))),
    }


masked_score = -1e+30

def time_core(query, key_ext, value_ext, band_width, first_row):
    series_count, block_rows, row_width = query.shape
    head_count = band_width.shape[0]
    head_depth = row_width // head_count
    border_rows = key_ext.shape[1] - block_rows
    query_heads = query.reshape(series_count, block_rows, head_count, head_depth)
    key_heads = key_ext.reshape(series_count, block_rows + border_rows, head_count, head_depth)
    value_heads = value_ext.reshape(series_count, block_rows + border_rows, head_count, head_depth)
    scores = jnp.einsum('sthd,sihd->shti', query_heads, key_heads, precision=lax.Precision.HIGHEST) * head_depth ** (-0.5)
    query_pos = lax.broadcasted_iota(jnp.int32, (block_rows, block_rows + border_rows), 0)
    key_pos = lax.broadcasted_iota(jnp.int32, (block_rows, block_rows + border_rows), 1)
    offset = query_pos + border_rows - key_pos
    absolute = first_row + key_pos - border_rows
    in_band = (offset[None] >= 0) & (offset[None] < band_width[:, None, None]) & (absolute[None] >= 0)
    scores = jnp.where(in_band[None], scores, masked_score)
    row_top = lax.stop_gradient(lax.optimization_barrier(jnp.max(scores, axis=-1, keepdims=True)))
    weights = jnp.exp(scores - row_top)
    probabilities = weights / lax.optimization_barrier(jnp.sum(weights, axis=-1, keepdims=True))
    probabilities = lax.optimization_barrier(probabilities.astype(jnp.bfloat16)).astype(jnp.float32)
    mixed = jnp.einsum('shti,sihd->sthd', probabilities, value_heads, precision=lax.Precision.HIGHEST)
    return mixed.reshape(series_count, block_rows, row_width).astype(jnp.bfloat16)

def group_core(query, key, value, query_ids, key_ids, head_depth):
    series_count, block_rows, row_width = query.shape
    key_count = key.shape[0]
    head_count = row_width // head_depth
    query_heads = query.reshape(series_count, block_rows, head_count, head_depth)
    key_heads = key.reshape(key_count, block_rows, head_count, head_depth)
    value_heads = value.reshape(key_count, block_rows, head_count, head_depth)
    scores = jnp.einsum('sthd,rthd->thsr', query_heads, key_heads, precision=lax.Precision.HIGHEST) * head_depth ** (-0.5)
    same_group = query_ids[:, None] == key_ids[None, :]
    scores = jnp.where(same_group[None, None], scores, masked_score)
    row_top = lax.stop_gradient(lax.optimization_barrier(jnp.max(scores, axis=-1, keepdims=True)))
    weights = jnp.exp(scores - row_top)
    probabilities = weights / lax.optimization_barrier(jnp.sum(weights, axis=-1, keepdims=True))
    probabilities = lax.optimization_barrier(probabilities.astype(jnp.bfloat16)).astype(jnp.float32)
    mixed = jnp.einsum('thsr,rthd->sthd', probabilities, value_heads, precision=lax.Precision.HIGHEST)
    return mixed.reshape(series_count, block_rows, row_width).astype(jnp.bfloat16)

def time_attention(query, key, value, band_width):
    series_count, total, row_width = query.shape
    blocks = N_TM
    block_rows = total // blocks
    border_rows = BAND - 1
    query_blocks = query.astype(jnp.float32).reshape(series_count, blocks, block_rows, row_width)
    key_blocks = key.astype(jnp.float32).reshape(series_count, blocks, block_rows, row_width)
    value_blocks = value.astype(jnp.float32).reshape(series_count, blocks, block_rows, row_width)

    def extend(blocked):
        tail = blocked[:, :, block_rows - border_rows:]
        tail = jnp.concatenate([jnp.zeros_like(tail[:, :1]), tail[:, :-1]], axis=1)
        return jnp.concatenate([tail, blocked], axis=2)
    key_ext = extend(key_blocks)
    value_ext = extend(value_blocks)
    firsts = jnp.arange(blocks, dtype=jnp.int32) * block_rows

    def one_block(inputs):
        return time_core(inputs[0], inputs[1], inputs[2], band_width, inputs[3])
    mixed = lax.map(jax.checkpoint(one_block), (jnp.moveaxis(query_blocks, 1, 0), jnp.moveaxis(key_ext, 1, 0), jnp.moveaxis(value_ext, 1, 0), firsts))
    return jnp.moveaxis(mixed, 0, 1).reshape(series_count, total, row_width)

def group_attention(query, key, value, series_group):
    series_count, total, row_width = query.shape
    blocks = N_TM
    block_rows = total // blocks

    def split_blocks(array):
        return jnp.moveaxis(array.astype(jnp.float32).reshape(series_count, blocks, block_rows, row_width), 1, 0)

    def one_block(inputs):
        return group_core(inputs[0], inputs[1], inputs[2], series_group, series_group, HEAD_DIM)
    mixed = lax.map(jax.checkpoint(one_block), (split_blocks(query), split_blocks(key), split_blocks(value)))
    return jnp.moveaxis(mixed, 0, 1).reshape(series_count, total, row_width)

def reference(time_query, time_key, time_value, group_query, group_key, group_value, out_time, out_group, series_group, band_width, cotangent):

    def forward(t_query, t_key, t_value, g_query, g_key, g_value):
        return (time_attention(t_query, t_key, t_value, band_width), group_attention(g_query, g_key, g_value, series_group))
    (time_out, group_out), pull_back = jax.vjp(forward, time_query, time_key, time_value, group_query, group_key, group_value)
    cot_flat = cotangent.reshape(-1, D)
    row_width = HEADS * HEAD_DIM

    def back_project(weight):
        product = lax.dot_general(cot_flat, weight, (((1,), (1,)), ((), ())), preferred_element_type=jnp.float32)
        return product.astype(jnp.bfloat16).reshape(SERIES, TIME, row_width)
    grads = pull_back((back_project(out_time), back_project(out_group)))
    grad_scale = (SERIES * TIME) ** (-0.5)
    grad_wt = lax.dot_general(time_out.reshape(-1, row_width), cot_flat, (((0,), (0,)), ((), ())), preferred_element_type=jnp.float32) * grad_scale
    grad_wg = lax.dot_general(group_out.reshape(-1, row_width), cot_flat, (((0,), (0,)), ((), ())), preferred_element_type=jnp.float32) * grad_scale
    return (grads[0], grads[1], grads[2], grads[3], grads[4], grads[5], grad_wt, grad_wg)
```

```python
import functools

import jax
import jax.numpy as jnp
import numpy as np
from jax import lax
from jax.experimental import pallas as pl
from jax.experimental.pallas import tpu as pltpu
from jax.sharding import PartitionSpec as P

HEAD_DIM = 64
BAND = 16
QUAD = 4
MASKED = -1e30
F32 = jnp.float32
BF16 = jnp.bfloat16
NT = (((1,), (1,)), ((), ()))
NN = (((1,), (0,)), ((), ()))
TN = (((0,), (0,)), ((), ()))


def dot(left, right, dims):
    return lax.dot_general(left, right, dims, preferred_element_type=F32)


def call(body, out_shape, operands, flops, size, smem=(), aliases=None, scratch=()):
    space = [
        pl.BlockSpec(memory_space=pltpu.SMEM if index in smem else pltpu.VMEM)
        for index in range(len(operands))
    ]
    single = isinstance(out_shape, jax.ShapeDtypeStruct)
    out_specs = (
        pl.BlockSpec(memory_space=pltpu.VMEM)
        if single
        else [pl.BlockSpec(memory_space=pltpu.VMEM)] * len(out_shape)
    )
    return pl.pallas_call(
        body,
        out_shape=out_shape,
        in_specs=space,
        out_specs=out_specs,
        scratch_shapes=list(scratch),
        input_output_aliases=aliases or {},
        compiler_params=pltpu.CompilerParams(vmem_limit_bytes=48 * 1024 * 1024),
        cost_estimate=pl.CostEstimate(flops=flops, bytes_accessed=size, transcendentals=0),
    )(*operands)


def shape(dims, dtype):
    return jax.ShapeDtypeStruct(dims, dtype)


def stacked(rows):
    lane = lax.broadcasted_iota(jnp.int32, rows.shape, 1) // HEAD_DIM
    zero = jnp.zeros_like(rows)
    return jnp.concatenate([jnp.where(lane == h, rows, zero) for h in range(QUAD)], axis=0)


def unstacked(rows):
    count = rows.shape[0] // QUAD
    low = lax.broadcasted_iota(jnp.int32, (count, 2 * HEAD_DIM), 1) < HEAD_DIM
    parts = []
    for pair in range(QUAD // 2):
        lanes = slice(2 * HEAD_DIM * pair, 2 * HEAD_DIM * (pair + 1))
        first = rows[2 * pair * count : (2 * pair + 1) * count, lanes]
        second = rows[(2 * pair + 1) * count : (2 * pair + 2) * count, lanes]
        parts.append(jnp.where(low, first, second))
    return jnp.concatenate(parts, axis=1)


def column_softmax(scores, keep):
    scores = jnp.where(keep, scores * HEAD_DIM ** (-0.5), MASKED)
    weights = jnp.exp(scores - jnp.max(scores, axis=0, keepdims=True))
    return weights * (1.0 / jnp.sum(weights, axis=0, keepdims=True))


def backward(prob, query_stack, key, value, grad_stack):
    grad_prob = dot(value, grad_stack, NT).astype(BF16).astype(F32)
    centred = grad_prob - jnp.sum(grad_prob * prob, axis=0, keepdims=True)
    grad_score = prob * centred * HEAD_DIM ** (-0.5)
    high = grad_score.astype(BF16)
    low = (grad_score - high.astype(F32)).astype(BF16)
    grad_query = dot(high, key, TN) + dot(low, key, TN)
    grad_key = dot(high, query_stack, NN) + dot(low, query_stack, NN)
    grad_value = dot(prob.astype(BF16), grad_stack, NN)
    return grad_query, grad_key, grad_value


def term_of(spread_ref, cot, mixed, scale, out_ref):
    rows = dot(spread_ref[...], cot, NT).astype(BF16)
    term = dot(rows, mixed, NN) * scale
    for part in range(out_ref.shape[0]):
        out_ref[part] = term[:, 128 * part : 128 * (part + 1)].astype(BF16)


def pack_body(q_ref, k_ref, v_ref, c_ref, out_ref):
    ser = q_ref.shape[0]
    start = 0
    for ref in (q_ref, k_ref, v_ref, c_ref):
        width = ref.shape[2]
        for s in range(ser):
            for j in range(out_ref.shape[0]):
                out_ref[j, 16 * s : 16 * (s + 1), start : start + width] = ref[
                    s, 16 * j : 16 * (j + 1), :
                ]
        start += width


def unpack_body(in_ref, q_ref, k_ref, v_ref):
    ser = q_ref.shape[0]
    for index, ref in enumerate((q_ref, k_ref, v_ref)):
        width = ref.shape[2]
        for s in range(ser):
            for j in range(in_ref.shape[0]):
                ref[s, 16 * j : 16 * (j + 1), :] = in_ref[
                    j, 16 * s : 16 * (s + 1), width * index : width * (index + 1)
                ]


def time_forward_body(
    scale, q_ref, k_ref, v_ref, rim_ref, c_ref, spread_ref, band_ref, first_ref, prob_ref, term_ref, mixed
):
    ser, rows, width = q_ref.shape
    keys = rows + BAND
    lanes = QUAD * HEAD_DIM
    key_pos = lax.broadcasted_iota(jnp.int32, (keys, QUAD * rows), 0)
    column = lax.broadcasted_iota(jnp.int32, (keys, QUAD * rows), 1)
    offset = lax.rem(column, rows) + BAND - key_pos
    head = column // rows
    inside = key_pos >= jnp.where(first_ref[0] == 0, BAND, 0)
    for quad in range(width // lanes):
        band = jnp.where(
            head < 2,
            jnp.where(head == 0, band_ref[QUAD * quad], band_ref[QUAD * quad + 1]),
            jnp.where(head == 2, band_ref[QUAD * quad + 2], band_ref[QUAD * quad + 3]),
        )
        keep = (offset >= 0) & (offset < band) & inside
        cut = slice(lanes * quad, lanes * (quad + 1))
        for s in range(ser):
            key = jnp.concatenate([rim_ref[0, s, :, cut], k_ref[s, :, cut]], axis=0)
            value = jnp.concatenate([rim_ref[1, s, :, cut], v_ref[s, :, cut]], axis=0)
            prob = column_softmax(dot(key, stacked(q_ref[s, :, cut]), NT), keep)
            prob_ref[s, quad] = prob
            out = unstacked(dot(prob.astype(BF16), value, TN))
            mixed[rows * s : rows * (s + 1), cut] = out.astype(BF16)
    cot = c_ref[...].reshape(ser * rows, c_ref.shape[2])
    term_of(spread_ref, cot, mixed[...], scale, term_ref)


def time_backward_body(
    prob_ref, q_ref, k_ref, v_ref, rim_ref, c_ref, w_ref, gq_ref, gk_ref, gv_ref, tail_ref, rimg_ref, grad
):
    ser, rows, width = q_ref.shape
    lanes = QUAD * HEAD_DIM
    cot = c_ref[...].reshape(ser * rows, c_ref.shape[2])
    for j in range(w_ref.shape[0]):
        grad[:, 128 * j : 128 * (j + 1)] = dot(cot, w_ref[j, :128, :], NT).astype(BF16)
    for quad in range(width // lanes):
        cut = slice(lanes * quad, lanes * (quad + 1))
        for s in range(ser):
            key = jnp.concatenate([rim_ref[0, s, :, cut], k_ref[s, :, cut]], axis=0)
            value = jnp.concatenate([rim_ref[1, s, :, cut], v_ref[s, :, cut]], axis=0)
            gq, gk, gv = backward(
                prob_ref[s, quad],
                stacked(q_ref[s, :, cut]),
                key,
                value,
                stacked(grad[rows * s : rows * (s + 1), cut]),
            )
            gq_ref[s, :, cut] = unstacked(gq).astype(BF16)
            for index, (result, ref) in enumerate(((gk, gk_ref), (gv, gv_ref))):
                rimg_ref[index, s, :, cut] = result[:BAND]
                ref[s, :, cut] = result[BAND:].astype(BF16)
                tail_ref[index, s, :, cut] = result[rows:]


def time_join_body(gk_in, gv_in, tail_ref, got_ref, gk_ref, gv_ref):
    rows = gk_in.shape[1]
    for index, (source, ref) in enumerate(((gk_in, gk_ref), (gv_in, gv_ref))):
        ref[:, : rows - BAND, :] = source[:, : rows - BAND, :]
        ref[:, rows - BAND :, :] = (tail_ref[index] + got_ref[index]).astype(BF16)


def group_body(scale, x_ref, w_ref, spread_ref, idk_ref, idq_ref, out_ref, term_ref, grad, mixed, res):
    total = x_ref.shape[0]
    patches = 16
    series = total // patches
    width = w_ref.shape[0] * 128
    lanes = QUAD * HEAD_DIM
    half = patches // 2
    cot = x_ref[:, 3 * width :]
    for j in range(w_ref.shape[0]):
        grad[:, 128 * j : 128 * (j + 1)] = dot(cot, w_ref[j, 128:, :], NT).astype(BF16)
    keep = idk_ref[...] == idq_ref[...]

    def rows_of(whole, part):
        cube = whole.astype(F32).reshape(series, patches, whole.shape[1])
        return cube[:, half * part : half * (part + 1)].reshape(-1, whole.shape[1]).astype(BF16)

    for quad in range(width // lanes):
        cut = [slice(width * n + lanes * quad, width * n + lanes * (quad + 1)) for n in range(3)]
        for part in range(2):
            query = stacked(rows_of(x_ref[:, cut[0]], part))
            key = rows_of(x_ref[:, cut[1]], part)
            value = rows_of(x_ref[:, cut[2]], part)
            prob = column_softmax(dot(key, query, NT), keep)
            out = unstacked(dot(prob.astype(BF16), value, TN))
            grad_stack = stacked(rows_of(grad[:, cut[0]], part))
            gq, gk, gv = backward(prob, query, key, value, grad_stack)
            place = slice(half * part, half * (part + 1))
            for index, result in enumerate((unstacked(gq), gk, gv, out)):
                spot = slice(width * index + lanes * quad, width * index + lanes * (quad + 1))
                res[:, place, spot] = result.reshape(series, half, lanes)
    out_ref[...] = res[:, :, : 3 * width].reshape(total, 3 * width).astype(BF16)
    mixed[...] = res[:, :, 3 * width :].reshape(total, width).astype(BF16)
    term_of(spread_ref, cot, mixed[...], scale, term_ref)


def sum_body(in_ref, out_ref):
    chunks = in_ref.shape[0] // 8
    total = jnp.sum(in_ref[...].astype(F32).reshape(chunks, 8, 128), axis=0)
    out_ref[...] = jnp.transpose(total)[:, : out_ref.shape[1]]


def per_device(
    time_query,
    time_key,
    time_value,
    group_query,
    group_key,
    group_value,
    out_time,
    out_group,
    series_group,
    band_width,
    cotangent,
):
    ser, rows, width = time_query.shape
    model = cotangent.shape[2]
    parts = lax.axis_size("series")
    count = lax.axis_size("tm")
    columns = model // count
    scale = float(ser * parts * rows * count) ** (-0.5)
    place = lax.axis_index("tm")
    patches = rows // parts

    rim = jnp.stack([time_key[:, rows - BAND :], time_value[:, rows - BAND :]])
    rim = lax.ppermute(rim, "tm", [(i, i + 1) for i in range(count - 1)])

    packed = call(
        pack_body,
        shape((parts, ser * patches, 3 * width + model), BF16),
        (group_query, group_key, group_value, cotangent),
        0,
        3_000_000,
    )
    moved = lax.all_to_all(packed, "series", 0, 0, tiled=True)
    weights = lax.all_gather(jnp.concatenate([out_time, out_group], axis=0), "series", axis=0)

    spread = np.zeros((8 * count, model), np.float32)
    for i in range(count):
        for e in range(columns):
            spread[8 * i + e, columns * i + e] = 1
    spread = jnp.asarray(spread, BF16)

    ident = series_group[:, None] * (patches // 2) + jnp.arange(patches // 2, dtype=jnp.int32)[None]
    ident = ident.reshape(-1)
    id_key = ident[:, None]
    id_query = jnp.tile(ident, QUAD)[None]

    quads = width // (QUAD * HEAD_DIM)
    prob, term_time = call(
        functools.partial(time_forward_body, scale),
        (
            shape((ser, quads, rows + BAND, QUAD * rows), F32),
            shape((parts, 8 * count, 128), BF16),
        ),
        (time_query, time_key, time_value, rim, cotangent, spread, band_width, place.reshape(1)),
        2_000_000_000,
        6_000_000,
        smem=(6, 7),
        scratch=[pltpu.VMEM((ser * rows, width), BF16)],
    )
    got_time = lax.all_to_all(
        term_time.reshape(parts * count, 8, 128), ("series", "tm"), 0, 0, tiled=True
    )
    grad_wt = call(
        sum_body, shape((128, columns), F32), (got_time.reshape(-1, 128),), 0, 1_000_000
    )

    back, term_group = call(
        functools.partial(group_body, scale),
        (
            shape((parts * ser * patches, 3 * width), BF16),
            shape((parts, 8 * count, 128), BF16),
        ),
        (
            moved.reshape(parts * ser * patches, 3 * width + model),
            weights,
            spread,
            id_key,
            id_query,
        ),
        4_000_000_000,
        6_000_000,
        scratch=[
            pltpu.VMEM((parts * ser * patches, width), BF16),
            pltpu.VMEM((parts * ser * patches, width), BF16),
            pltpu.VMEM((parts * ser, patches, 4 * width), F32),
        ],
    )
    returned = lax.all_to_all(
        back.reshape(parts, ser * patches, 3 * width), "series", 0, 0, tiled=True
    )
    got_group = lax.all_to_all(
        term_group.reshape(parts * count, 8, 128), ("series", "tm"), 0, 0, tiled=True
    )

    grad_tq, grad_tk, grad_tv, tail, rim_grad = call(
        time_backward_body,
        (
            shape((ser, rows, width), BF16),
            shape((ser, rows, width), BF16),
            shape((ser, rows, width), BF16),
            shape((2, ser, BAND, width), F32),
            shape((2, ser, BAND, width), F32),
        ),
        (prob, time_query, time_key, time_value, rim, cotangent, weights),
        2_000_000_000,
        6_000_000,
        scratch=[pltpu.VMEM((ser * rows, width), BF16)],
    )
    rim_back = lax.ppermute(rim_grad, "tm", [(i + 1, i) for i in range(count - 1)])
    grad_tk, grad_tv = call(
        time_join_body,
        (shape((ser, rows, width), BF16), shape((ser, rows, width), BF16)),
        (grad_tk, grad_tv, tail, rim_back),
        0,
        2_000_000,
    )
    grad_wg = call(
        sum_body, shape((128, columns), F32), (got_group.reshape(-1, 128),), 0, 1_000_000
    )
    grad_gq, grad_gk, grad_gv = call(
        unpack_body,
        (shape((ser, rows, width), BF16),) * 3,
        (returned,),
        0,
        2_000_000,
    )
    return (grad_tq, grad_tk, grad_tv, grad_gq, grad_gk, grad_gv, grad_wt, grad_wg)


def solution(mesh):
    rows = P("series", "tm", None)
    return jax.shard_map(
        per_device,
        mesh=mesh,
        in_specs=(rows,) * 6 + (P("series", None),) * 2 + (P(), P(), rows),
        out_specs=(rows,) * 6 + (P("series", "tm"),) * 2,
        check_vma=False,
    )
```

```python
import functools

import jax
import jax.numpy as jnp
import numpy as np
from jax import lax
from jax.experimental import pallas as pl
from jax.experimental.pallas import tpu as pltpu
from jax.sharding import PartitionSpec as P

HEAD_DIM = 64
BAND = 16
QUAD = 4
X_SIZE, Y_SIZE, LOW_SIZE = 4, 8, 2
MASKED = -1e30
F32 = jnp.float32
BF16 = jnp.bfloat16
NT = (((1,), (1,)), ((), ()))
NN = (((1,), (0,)), ((), ()))
TN = (((0,), (0,)), ((), ()))


def dot(left, right, dims):
    return lax.dot_general(left, right, dims, preferred_element_type=F32)


def block(operand, where):
    if where == "smem":
        return pl.BlockSpec(memory_space=pltpu.SMEM)
    if where == "any":
        return pl.BlockSpec(memory_space=pl.ANY)
    zeros = (0,) * len(operand.shape)
    return pl.BlockSpec(operand.shape, lambda i: zeros)


def call(body, out_shape, operands, flops, size, smem=(), anywhere=False, scratch=(), room=60 * 1024):
    usual = "any" if anywhere else "vmem"
    many = isinstance(out_shape, (tuple, list))
    outs = [block(o, usual) for o in out_shape] if many else block(out_shape, usual)
    return pl.pallas_call(
        body,
        out_shape=out_shape,
        grid=(1,),
        in_specs=[block(o, "smem" if n in smem else usual) for n, o in enumerate(operands)],
        out_specs=outs,
        scratch_shapes=list(scratch),
        compiler_params=pltpu.CompilerParams(vmem_limit_bytes=room * 1024),
        cost_estimate=pl.CostEstimate(flops=flops, bytes_accessed=size, transcendentals=0),
    )(*operands)


def shape(dims, dtype):
    return jax.ShapeDtypeStruct(dims, dtype)


def stacked(rows):
    lane = lax.broadcasted_iota(jnp.int32, rows.shape, 1) // HEAD_DIM
    zero = jnp.zeros_like(rows)
    return jnp.concatenate([jnp.where(lane == h, rows, zero) for h in range(QUAD)], axis=0)


def unstacked(rows):
    count = rows.shape[0] // QUAD
    low = lax.broadcasted_iota(jnp.int32, (count, 2 * HEAD_DIM), 1) < HEAD_DIM
    parts = []
    for pair in range(QUAD // 2):
        lanes = slice(2 * HEAD_DIM * pair, 2 * HEAD_DIM * (pair + 1))
        first = rows[2 * pair * count : (2 * pair + 1) * count, lanes]
        second = rows[(2 * pair + 1) * count : (2 * pair + 2) * count, lanes]
        parts.append(jnp.where(low, first, second))
    return jnp.concatenate(parts, axis=1)


def column_softmax(scores, keep):
    scores = jnp.where(keep, scores * HEAD_DIM ** (-0.5), MASKED)
    weights = jnp.exp(scores - jnp.max(scores, axis=0, keepdims=True))
    return weights * (1.0 / jnp.sum(weights, axis=0, keepdims=True))


def backward(prob, query_stack, key, value, grad_stack):
    grad_prob = dot(value, grad_stack, NT).astype(BF16).astype(F32)
    centred = grad_prob - jnp.sum(grad_prob * prob, axis=0, keepdims=True)
    grad_score = prob * centred * HEAD_DIM ** (-0.5)
    high = grad_score.astype(BF16)
    low = (grad_score - high.astype(F32)).astype(BF16)
    grad_query = dot(high, key, TN) + dot(low, key, TN)
    grad_key = dot(high, query_stack, NN) + dot(low, query_stack, NN)
    grad_value = dot(prob.astype(BF16), grad_stack, NN)
    return grad_query, grad_key, grad_value


def term_of(spread_ref, cot, mixed, scale):
    rows = dot(spread_ref[...], cot, NT).astype(BF16)
    return (dot(rows, mixed, NN) * scale).astype(BF16)


def x_of(place_ref):
    return lax.rem(place_ref[1] // (2 * Y_SIZE), X_SIZE)


def core_of(place_ref):
    return lax.rem(place_ref[1], 2)


def run_copies(copies):
    for copy in copies:
        copy.start()
    for copy in copies:
        copy.wait()


def pack_body(q_ref, k_ref, v_ref, c_ref, out_ref):
    start = 0
    for ref in (q_ref, k_ref, v_ref, c_ref):
        width = ref.shape[2]
        for target in range(out_ref.shape[0]):
            out_ref[target, :, :, start : start + width] = ref[:, 16 * target : 16 * (target + 1)]
        start += width


def piece_body(place_ref, wt_ref, wg_ref, out_ref):
    rows = out_ref.shape[1]
    spot = pl.ds(pl.multiple_of(rows * x_of(place_ref), rows), rows)
    piece = jnp.where(core_of(place_ref) == 0, wt_ref[spot], wg_ref[spot])
    for j in range(out_ref.shape[0]):
        out_ref[j] = piece


def gather_body(place_ref, *rest):
    blocks, out_ref, sems = rest[:-2], rest[-2], rest[-1]
    count = len(blocks)
    copies = []
    for shift, ref in enumerate(blocks):
        source = lax.rem(x_of(place_ref) + count - shift, count)
        copies.append(pltpu.make_async_copy(ref, out_ref.at[source], sems.at[shift]))
    run_copies(copies)


def unpack_body(place_ref, *rest):
    blocks, outs, sems = rest[:-4], rest[-4:-1], rest[-1]
    count = len(blocks)
    copies = []
    for shift, ref in enumerate(blocks):
        source = lax.rem(place_ref[0] + shift, count)
        for index, out_ref in enumerate(outs):
            width = out_ref.shape[2]
            copies.append(
                pltpu.make_async_copy(
                    ref.at[:, :, pl.ds(width * index, width)],
                    out_ref.at[:, pl.ds(pl.multiple_of(16 * source, 16), 16), :],
                    sems.at[len(copies)],
                )
            )
    run_copies(copies)


def time_forward_body(
    scale, place_ref, band_ref, q_ref, k_ref, v_ref, rim_ref, c_ref, spread_ref, prob_ref, term_ref, mixed
):
    ser, rows, width = q_ref.shape
    keys = rows + BAND
    lanes = QUAD * HEAD_DIM
    key_pos = lax.broadcasted_iota(jnp.int32, (keys, QUAD * rows), 0)
    column = lax.broadcasted_iota(jnp.int32, (keys, QUAD * rows), 1)
    offset = lax.rem(column, rows) + BAND - key_pos
    head = column // rows
    inside = key_pos >= jnp.where(place_ref[1] == 0, BAND, 0)
    for quad in range(width // lanes):
        band = jnp.where(
            head < 2,
            jnp.where(head == 0, band_ref[QUAD * quad], band_ref[QUAD * quad + 1]),
            jnp.where(head == 2, band_ref[QUAD * quad + 2], band_ref[QUAD * quad + 3]),
        )
        keep = (offset >= 0) & (offset < band) & inside
        cut = slice(lanes * quad, lanes * (quad + 1))
        for s in range(ser):
            key = jnp.concatenate([rim_ref[0, s, :, cut], k_ref[s, :, cut]], axis=0)
            value = jnp.concatenate([rim_ref[1, s, :, cut], v_ref[s, :, cut]], axis=0)
            prob = column_softmax(dot(key, stacked(q_ref[s, :, cut]), NT), keep)
            prob_ref[s, quad] = prob
            out = unstacked(dot(prob.astype(BF16), value, TN))
            mixed[rows * s : rows * (s + 1), cut] = out.astype(BF16)
    cot = c_ref[...].reshape(ser * rows, c_ref.shape[2])
    term_ref[...] = term_of(spread_ref, cot, mixed[...], scale)


def back_project(cot, own, mine_ref, other_ref, weights, grad):
    xs, parts, rows, _ = mine_ref.shape
    for x in range(xs):
        for j in range(parts):
            start = rows * (xs * j + x)
            weights[start : start + rows] = jnp.where(own, mine_ref[x, j], other_ref[x, j])
    grad[...] = dot(cot, weights[...], NT).astype(BF16)


def time_backward_body(
    place_ref, prob_ref, q_ref, k_ref, v_ref, rim_ref, c_ref, mine_ref, other_ref,
    gq_ref, gk_ref, gv_ref, tail_ref, rimg_ref, grad, weights
):
    ser, rows, width = q_ref.shape
    lanes = QUAD * HEAD_DIM
    cot = c_ref[...].reshape(ser * rows, c_ref.shape[2])
    back_project(cot, core_of(place_ref) == 0, mine_ref, other_ref, weights, grad)
    for quad in range(width // lanes):
        cut = slice(lanes * quad, lanes * (quad + 1))
        for s in range(ser):
            key = jnp.concatenate([rim_ref[0, s, :, cut], k_ref[s, :, cut]], axis=0)
            value = jnp.concatenate([rim_ref[1, s, :, cut], v_ref[s, :, cut]], axis=0)
            gq, gk, gv = backward(
                prob_ref[s, quad],
                stacked(q_ref[s, :, cut]),
                key,
                value,
                stacked(grad[rows * s : rows * (s + 1), cut]),
            )
            gq_ref[s, :, cut] = unstacked(gq).astype(BF16)
            for index, (result, ref) in enumerate(((gk, gk_ref), (gv, gv_ref))):
                rimg_ref[index, s, :, cut] = result[:BAND].astype(BF16)
                ref[s, :, cut] = result[BAND:].astype(BF16)
                tail_ref[index, s, :, cut] = result[rows:]


def time_join_body(gk_any, gv_any, tail_ref, got_ref, gk_ref, gv_ref):
    for index, ref in enumerate((gk_ref, gv_ref)):
        ref[...] = (tail_ref[index] + got_ref[index].astype(F32)).astype(BF16)


def group_ids(group_ref, series, patch, count, half):
    ids = jnp.zeros_like(series)
    for s in range(count):
        ids = jnp.where(series == s, group_ref[s], ids)
    return ids * half + patch


def half_rows(cube, part):
    half = cube.shape[1] // 2
    cube = cube.astype(F32)[:, half * part : half * (part + 1)]
    return cube.reshape(-1, cube.shape[2]).astype(BF16)


def moved_rows(x_ref, lane, part):
    parts, ser, patches, _ = x_ref.shape
    lanes = QUAD * HEAD_DIM
    cube = x_ref[:, :, :, lane : lane + lanes].reshape(parts * ser, patches, lanes)
    return half_rows(cube, part)


def group_forward_body(
    scale, group_ref, x_ref, spread_ref, time_term_ref, prob_ref, term_ref, mixed, res
):
    parts, ser, patches, _ = x_ref.shape
    series = parts * ser
    width = mixed.shape[1]
    lanes = QUAD * HEAD_DIM
    half = patches // 2
    count = series * half
    row = lax.broadcasted_iota(jnp.int32, (count, 1), 0)
    column = lax.rem(lax.broadcasted_iota(jnp.int32, (1, QUAD * count), 1), count)
    id_key = group_ids(group_ref, row // half, lax.rem(row, half), series, half)
    id_query = group_ids(group_ref, column // half, lax.rem(column, half), series, half)
    keep = id_key == id_query
    for quad in range(width // lanes):
        start = lanes * quad
        for part in range(2):
            query = stacked(moved_rows(x_ref, start, part))
            key = moved_rows(x_ref, width + start, part)
            value = moved_rows(x_ref, 2 * width + start, part)
            prob = column_softmax(dot(key, query, NT), keep)
            prob_ref[quad, part] = prob
            out = unstacked(dot(prob.astype(BF16), value, TN))
            res[:, half * part : half * (part + 1), start : start + lanes] = out.reshape(
                series, half, lanes
            )
    mixed[...] = res[...].reshape(series * patches, width).astype(BF16)
    cot = x_ref[:, :, :, 3 * width :].reshape(series * patches, spread_ref.shape[1])
    term_ref[:, :width] = time_term_ref[...]
    term_ref[:, width:] = term_of(spread_ref, cot, mixed[...], scale)


def group_backward_body(place_ref, x_ref, prob_ref, mine_ref, other_ref, *rest):
    outs, (grad, weights, res) = rest[:-3], rest[-3:]
    parts, ser, patches, _ = x_ref.shape
    series = parts * ser
    width = grad.shape[1]
    lanes = QUAD * HEAD_DIM
    half = patches // 2
    cot = x_ref[:, :, :, 3 * width :].reshape(series * patches, weights.shape[1])
    back_project(cot, core_of(place_ref) == 1, mine_ref, other_ref, weights, grad)
    for quad in range(width // lanes):
        start = lanes * quad
        for part in range(2):
            query = stacked(moved_rows(x_ref, start, part))
            key = moved_rows(x_ref, width + start, part)
            value = moved_rows(x_ref, 2 * width + start, part)
            own_grad = grad[:, start : start + lanes].reshape(series, patches, lanes)
            grad_stack = stacked(half_rows(own_grad, part))
            gq, gk, gv = backward(prob_ref[quad, part], query, key, value, grad_stack)
            for index, result in enumerate((unstacked(gq), gk, gv)):
                spot = slice(width * index + start, width * index + start + lanes)
                res[:, half * part : half * (part + 1), spot] = result.reshape(series, half, lanes)
    for shift, out_ref in enumerate(outs):
        source = lax.rem(place_ref[0] + parts - shift, parts)
        out_ref[...] = res[pl.ds(ser * source, ser)].astype(BF16)


def first_sum_body(pad_ref, in_ref, out_ref):
    total = jnp.sum(in_ref[...].astype(F32), axis=0).astype(BF16)
    total = dot(pad_ref[...], total, NN)
    lows = total.shape[0] // 8
    width = total.shape[1] // 2
    for j in range(width // 128):
        chunks = [
            total[:, start : start + 128].reshape(lows, 8, 128)
            for start in (128 * j, width + 128 * j)
        ]
        out_ref[lows * j : lows * (j + 1)] = jnp.concatenate(chunks, axis=1).astype(BF16)


def last_sum_body(in_ref, time_ref, group_ref):
    total = jnp.sum(in_ref[...].astype(F32), axis=0)
    columns = time_ref.shape[0]
    time_ref[...] = total[:columns]
    group_ref[...] = total[8 : 8 + columns]


def tm_index(low, x, y, core):
    return ((low * X_SIZE + x) * Y_SIZE + y) * 2 + core


def first_groups():
    return [
        [tm_index(low, x, y, core) for x in range(X_SIZE) for core in range(2)]
        for low in range(LOW_SIZE)
        for y in range(Y_SIZE)
    ]


def along_x(shift):
    return [
        (tm_index(low, x, y, core), tm_index(low, (x + shift) % X_SIZE, y, core))
        for low in range(LOW_SIZE)
        for x in range(X_SIZE)
        for y in range(Y_SIZE)
        for core in range(2)
    ]


def second_groups(parts, count):
    return [
        [
            j * count + tm_index(low, x, y, core)
            for j in range(parts)
            for y in range(Y_SIZE)
            for low in range(LOW_SIZE)
        ]
        for x in range(X_SIZE)
        for core in range(2)
    ]


def spread_matrix(model, count):
    columns = model // count
    order = [
        columns * tm_index(low, x, y, core) + e
        for x in range(X_SIZE)
        for core in range(2)
        for y in range(Y_SIZE)
        for low in range(LOW_SIZE)
        for e in range(columns)
    ]
    return jnp.asarray(np.eye(model, dtype=np.float32)[order], BF16)


def pad_matrix(columns):
    lows = Y_SIZE * LOW_SIZE
    pad = np.zeros((lows, 8, lows, columns), np.float32)
    for low in range(lows):
        for e in range(columns):
            pad[low, e, low, e] = 1
    return jnp.asarray(pad.reshape(8 * lows, columns * lows), BF16)


def per_device(
    time_query,
    time_key,
    time_value,
    group_query,
    group_key,
    group_value,
    out_time,
    out_group,
    series_group,
    band_width,
    cotangent,
):
    ser, rows, width = time_query.shape
    model = cotangent.shape[2]
    parts = lax.axis_size("series")
    count = lax.axis_size("tm")
    columns = model // count
    scale = float(ser * parts * rows * count) ** (-0.5)
    place = lax.axis_index("tm")
    patches = rows // parts

    series = lax.axis_index("series")
    where = jnp.stack([series, place]).astype(jnp.int32)

    def over_series(value, shift):
        return lax.ppermute(value, "series", [(j, (j + shift) % parts) for j in range(parts)])

    sem = pltpu.SemaphoreType.DMA
    piece_rows = out_time.shape[0] // X_SIZE
    piece = call(
        piece_body,
        shape((parts, piece_rows, model), BF16),
        (where, out_time, out_group),
        0,
        500_000,
        smem=(0,),
    )
    column_piece = lax.all_to_all(piece, "series", 0, 0, tiled=True)
    rim = jnp.stack([time_key[:, rows - BAND :], time_value[:, rows - BAND :]])
    rim = lax.ppermute(rim, "tm", [(i, i + 1) for i in range(count - 1)])
    packed = call(
        pack_body,
        shape((parts, ser, patches, 3 * width + model), BF16),
        (group_query, group_key, group_value, cotangent),
        0,
        3_000_000,
    )
    packed, column_piece, rim = lax.optimization_barrier((packed, column_piece, rim))
    moved = lax.all_to_all(packed, "series", 0, 0, tiled=True)
    spread = spread_matrix(model, count)
    quads = width // (QUAD * HEAD_DIM)
    prob, term_time = call(
        functools.partial(time_forward_body, scale),
        (
            shape((ser, quads, rows + BAND, QUAD * rows), F32),
            shape((model, width), BF16),
        ),
        (where, band_width, time_query, time_key, time_value, rim, cotangent, spread),
        2_000_000_000,
        6_000_000,
        smem=(0, 1),
        scratch=[pltpu.VMEM((ser * rows, width), BF16)],
    )
    pieces = [column_piece] + [
        lax.ppermute(column_piece, "tm", along_x(shift)) for shift in range(1, X_SIZE)
    ]
    order, term_time = lax.optimization_barrier((where, term_time))
    weight_mine = call(
        gather_body,
        shape((X_SIZE, parts, piece_rows, model), BF16),
        (order, *pieces),
        0,
        1_600_000,
        smem=(0,),
        anywhere=True,
        scratch=[sem((X_SIZE,))],
        room=8192,
    )
    weight_other = lax.ppermute(weight_mine, "tm", [(i, i ^ 1) for i in range(count)])

    grad_tq, grad_tk, grad_tv, tail, rim_grad = call(
        time_backward_body,
        (
            shape((ser, rows, width), BF16),
            shape((ser, rows, width), BF16),
            shape((ser, rows, width), BF16),
            shape((2, ser, BAND, width), F32),
            shape((2, ser, BAND, width), BF16),
        ),
        (
            where,
            prob,
            time_query,
            time_key,
            time_value,
            rim,
            cotangent,
            weight_mine,
            weight_other,
        ),
        4_000_000_000,
        6_000_000,
        smem=(0,),
        scratch=[pltpu.VMEM((ser * rows, width), BF16), pltpu.VMEM((width, model), BF16)],
    )
    rim_back = lax.ppermute(rim_grad, "tm", [(i + 1, i) for i in range(count - 1)])
    term_time, grad_tq = lax.optimization_barrier((term_time, grad_tq))
    total = parts * ser * patches
    group_prob, term = call(
        functools.partial(group_forward_body, scale),
        (
            shape((quads, 2, total // 2, QUAD * total // 2), F32),
            shape((model, 2 * width), BF16),
        ),
        (series_group, moved, spread, term_time),
        4_000_000_000,
        8_000_000,
        smem=(0,),
        scratch=[
            pltpu.VMEM((total, width), BF16),
            pltpu.VMEM((parts * ser, patches, width), F32),
        ],
    )
    first = 2 * X_SIZE
    plane = lax.all_to_all(
        term.reshape(first, model // first, 2 * width),
        "tm",
        0,
        0,
        tiled=True,
        axis_index_groups=first_groups(),
    )
    back = call(
        group_backward_body,
        (shape((ser, patches, 3 * width), BF16),) * parts,
        (where, moved, group_prob, weight_mine, weight_other),
        40_000_000_000,
        8_000_000,
        smem=(0,),
        scratch=[
            pltpu.VMEM((total, width), BF16),
            pltpu.VMEM((width, model), BF16),
            pltpu.VMEM((parts * ser, patches, 3 * width), F32),
        ],
    )
    plane, _ = lax.optimization_barrier((plane, back[0]))
    second = parts * Y_SIZE * LOW_SIZE
    chunks = call(
        first_sum_body,
        shape((second, 16, 128), BF16),
        (pad_matrix(columns), plane),
        0,
        500_000,
        room=8192,
    )
    returned = [back[0]] + [over_series(back[shift], -shift) for shift in range(1, parts)]

    chunks, tail = lax.optimization_barrier((chunks, tail))
    border = pl.BlockSpec((ser, BAND, width), lambda i: (0, rows // BAND - 1, 0))
    grad_tk, grad_tv = pl.pallas_call(
        time_join_body,
        out_shape=(shape((ser, rows, width), BF16),) * 2,
        grid=(1,),
        in_specs=[pl.BlockSpec(memory_space=pl.ANY)] * 2 + [block(tail, ""), block(rim_back, "")],
        out_specs=[border] * 2,
        input_output_aliases={0: 0, 1: 1},
        compiler_params=pltpu.CompilerParams(vmem_limit_bytes=60 * 1024 * 1024),
        cost_estimate=pl.CostEstimate(flops=40_000_000_000, bytes_accessed=1_000_000, transcendentals=0),
    )(grad_tk, grad_tv, tail, rim_back)
    order, grad_tk = lax.optimization_barrier((where, grad_tk))
    grad_gq, grad_gk, grad_gv = call(
        unpack_body,
        (shape((ser, rows, width), BF16),) * 3,
        (order, *returned),
        0,
        2_000_000,
        smem=(0,),
        anywhere=True,
        scratch=[sem((3 * parts,))],
        room=8192,
    )
    chunks = lax.all_to_all(
        chunks,
        ("series", "tm"),
        0,
        0,
        tiled=True,
        axis_index_groups=second_groups(parts, count),
    )
    grad_wt, grad_wg = call(
        last_sum_body, (shape((columns, 128), F32),) * 2, (chunks,), 0, 100_000, room=8192
    )
    return (grad_tq, grad_tk, grad_tv, grad_gq, grad_gk, grad_gv, grad_wt.T, grad_wg.T)


def solution(mesh):
    rows = P("series", "tm", None)
    return jax.shard_map(
        per_device,
        mesh=mesh,
        in_specs=(rows,) * 6 + (P("series", None),) * 2 + (P(), P(), rows),
        out_specs=(rows,) * 6 + (P("series", "tm"),) * 2,
        check_vma=False,
    )
```

```python
import functools

import jax
import jax.numpy as jnp
import numpy as np
from jax import lax
from jax.experimental import pallas as pl
from jax.experimental.pallas import tpu as pltpu
from jax.sharding import PartitionSpec as P

HEAD_DIM = 64
BAND = 16
QUAD = 4
X_SIZE, Y_SIZE, LOW_SIZE = 4, 8, 2
MASKED = -1e30
F32 = jnp.float32
BF16 = jnp.bfloat16
NT = (((1,), (1,)), ((), ()))
NN = (((1,), (0,)), ((), ()))
TN = (((0,), (0,)), ((), ()))


def dot(left, right, dims):
    return lax.dot_general(left, right, dims, preferred_element_type=F32)


def block(operand, where):
    if where == "smem":
        return pl.BlockSpec(memory_space=pltpu.SMEM)
    if where == "any":
        return pl.BlockSpec(memory_space=pl.ANY)
    zeros = (0,) * len(operand.shape)
    return pl.BlockSpec(operand.shape, lambda i: zeros)


def call(body, out_shape, operands, flops, size, smem=(), anywhere=False, scratch=(), room=60 * 1024):
    usual = "any" if anywhere else "vmem"
    many = isinstance(out_shape, (tuple, list))
    outs = [block(o, usual) for o in out_shape] if many else block(out_shape, usual)
    return pl.pallas_call(
        body,
        out_shape=out_shape,
        grid=(1,),
        in_specs=[block(o, "smem" if n in smem else usual) for n, o in enumerate(operands)],
        out_specs=outs,
        scratch_shapes=list(scratch),
        compiler_params=pltpu.CompilerParams(vmem_limit_bytes=room * 1024),
        cost_estimate=pl.CostEstimate(flops=flops, bytes_accessed=size, transcendentals=0),
    )(*operands)


def shape(dims, dtype):
    return jax.ShapeDtypeStruct(dims, dtype)


def stacked(rows):
    lane = lax.broadcasted_iota(jnp.int32, rows.shape, 1) // HEAD_DIM
    zero = jnp.zeros_like(rows)
    return jnp.concatenate([jnp.where(lane == h, rows, zero) for h in range(QUAD)], axis=0)


def unstacked(rows):
    count = rows.shape[0] // QUAD
    low = lax.broadcasted_iota(jnp.int32, (count, 2 * HEAD_DIM), 1) < HEAD_DIM
    parts = []
    for pair in range(QUAD // 2):
        lanes = slice(2 * HEAD_DIM * pair, 2 * HEAD_DIM * (pair + 1))
        first = rows[2 * pair * count : (2 * pair + 1) * count, lanes]
        second = rows[(2 * pair + 1) * count : (2 * pair + 2) * count, lanes]
        parts.append(jnp.where(low, first, second))
    return jnp.concatenate(parts, axis=1)


def column_softmax(scores, keep):
    scores = jnp.where(keep, scores * HEAD_DIM ** (-0.5), MASKED)
    weights = jnp.exp(scores - jnp.max(scores, axis=0, keepdims=True))
    return weights * (1.0 / jnp.sum(weights, axis=0, keepdims=True))


def backward(prob, query_stack, key, value, grad_stack):
    grad_prob = dot(value, grad_stack, NT).astype(BF16).astype(F32)
    centred = grad_prob - jnp.sum(grad_prob * prob, axis=0, keepdims=True)
    grad_score = prob * centred * HEAD_DIM ** (-0.5)
    high = grad_score.astype(BF16)
    low = (grad_score - high.astype(F32)).astype(BF16)
    grad_query = dot(high, key, TN) + dot(low, key, TN)
    grad_key = dot(high, query_stack, NN) + dot(low, query_stack, NN)
    grad_value = dot(prob.astype(BF16), grad_stack, NN)
    return grad_query, grad_key, grad_value


def term_of(spread_ref, cot, mixed, scale):
    rows = dot(spread_ref[...], cot, NT).astype(BF16)
    return (dot(rows, mixed, NN) * scale).astype(BF16)


def x_of(place_ref):
    return lax.rem(place_ref[1] // (2 * Y_SIZE), X_SIZE)


def core_of(place_ref):
    return lax.rem(place_ref[1], 2)


def run_copies(copies):
    for copy in copies:
        copy.start()
    for copy in copies:
        copy.wait()


def pack_body(q_ref, k_ref, v_ref, c_ref, out_ref):
    start = 0
    for ref in (q_ref, k_ref, v_ref, c_ref):
        width = ref.shape[2]
        for target in range(out_ref.shape[0]):
            out_ref[target, :, :, start : start + width] = ref[:, 16 * target : 16 * (target + 1)]
        start += width


def piece_body(place_ref, wt_ref, wg_ref, out_ref):
    rows = out_ref.shape[1]
    spot = pl.ds(pl.multiple_of(rows * x_of(place_ref), rows), rows)
    piece = jnp.where(core_of(place_ref) == 0, wt_ref[spot], wg_ref[spot])
    for j in range(out_ref.shape[0]):
        out_ref[j] = piece


def gather_body(place_ref, *rest):
    blocks, out_ref, sems = rest[:-2], rest[-2], rest[-1]
    count = len(blocks)
    copies = []
    for shift, ref in enumerate(blocks):
        source = lax.rem(x_of(place_ref) + count - shift, count)
        copies.append(pltpu.make_async_copy(ref, out_ref.at[source], sems.at[shift]))
    run_copies(copies)


def unpack_body(place_ref, *rest):
    blocks, outs, sems = rest[:-4], rest[-4:-1], rest[-1]
    count = len(blocks)
    copies = []
    for shift, ref in enumerate(blocks):
        source = lax.rem(place_ref[0] + shift, count)
        for index, out_ref in enumerate(outs):
            width = out_ref.shape[2]
            copies.append(
                pltpu.make_async_copy(
                    ref.at[:, :, pl.ds(width * index, width)],
                    out_ref.at[:, pl.ds(pl.multiple_of(16 * source, 16), 16), :],
                    sems.at[len(copies)],
                )
            )
    run_copies(copies)


def time_forward_body(
    scale, place_ref, band_ref, q_ref, k_ref, v_ref, rim_ref, c_ref, spread_ref, prob_ref, term_ref, mixed
):
    ser, rows, width = q_ref.shape
    keys = rows + BAND
    lanes = QUAD * HEAD_DIM
    key_pos = lax.broadcasted_iota(jnp.int32, (keys, QUAD * rows), 0)
    column = lax.broadcasted_iota(jnp.int32, (keys, QUAD * rows), 1)
    offset = lax.rem(column, rows) + BAND - key_pos
    head = column // rows
    inside = key_pos >= jnp.where(place_ref[1] == 0, BAND, 0)
    for quad in range(width // lanes):
        band = jnp.where(
            head < 2,
            jnp.where(head == 0, band_ref[QUAD * quad], band_ref[QUAD * quad + 1]),
            jnp.where(head == 2, band_ref[QUAD * quad + 2], band_ref[QUAD * quad + 3]),
        )
        keep = (offset >= 0) & (offset < band) & inside
        cut = slice(lanes * quad, lanes * (quad + 1))
        for s in range(ser):
            key = jnp.concatenate([rim_ref[0, s, :, cut], k_ref[s, :, cut]], axis=0)
            value = jnp.concatenate([rim_ref[1, s, :, cut], v_ref[s, :, cut]], axis=0)
            prob = column_softmax(dot(key, stacked(q_ref[s, :, cut]), NT), keep)
            prob_ref[s, quad] = prob
            out = unstacked(dot(prob.astype(BF16), value, TN))
            mixed[rows * s : rows * (s + 1), cut] = out.astype(BF16)
    cot = c_ref[...].reshape(ser * rows, c_ref.shape[2])
    term_ref[...] = term_of(spread_ref, cot, mixed[...], scale)


def back_project(cot, own, mine_ref, other_ref, weights, grad):
    xs, parts, rows, _ = mine_ref.shape
    for x in range(xs):
        for j in range(parts):
            start = rows * (xs * j + x)
            weights[start : start + rows] = jnp.where(own, mine_ref[x, j], other_ref[x, j])
    grad[...] = dot(cot, weights[...], NT).astype(BF16)


def time_backward_body(
    place_ref, prob_ref, q_ref, k_ref, v_ref, rim_ref, c_ref, mine_ref, other_ref,
    gq_ref, gk_ref, gv_ref, tail_ref, rimg_ref, grad, weights
):
    ser, rows, width = q_ref.shape
    lanes = QUAD * HEAD_DIM
    cot = c_ref[...].reshape(ser * rows, c_ref.shape[2])
    back_project(cot, core_of(place_ref) == 0, mine_ref, other_ref, weights, grad)
    for quad in range(width // lanes):
        cut = slice(lanes * quad, lanes * (quad + 1))
        for s in range(ser):
            key = jnp.concatenate([rim_ref[0, s, :, cut], k_ref[s, :, cut]], axis=0)
            value = jnp.concatenate([rim_ref[1, s, :, cut], v_ref[s, :, cut]], axis=0)
            gq, gk, gv = backward(
                prob_ref[s, quad],
                stacked(q_ref[s, :, cut]),
                key,
                value,
                stacked(grad[rows * s : rows * (s + 1), cut]),
            )
            gq_ref[s, :, cut] = unstacked(gq).astype(BF16)
            for index, (result, ref) in enumerate(((gk, gk_ref), (gv, gv_ref))):
                rimg_ref[index, s, :, cut] = result[:BAND].astype(BF16)
                ref[s, :, cut] = result[BAND:].astype(BF16)
                tail_ref[index, s, :, cut] = result[rows:]


def time_join_body(gk_any, gv_any, tail_ref, got_ref, gk_ref, gv_ref):
    for index, ref in enumerate((gk_ref, gv_ref)):
        ref[...] = (tail_ref[index] + got_ref[index].astype(F32)).astype(BF16)


def group_ids(group_ref, series, patch, count, half):
    ids = jnp.zeros_like(series)
    for s in range(count):
        ids = jnp.where(series == s, group_ref[s], ids)
    return ids * half + patch


def half_rows(cube, part):
    half = cube.shape[1] // 2
    cube = cube.astype(F32)[:, half * part : half * (part + 1)]
    return cube.reshape(-1, cube.shape[2]).astype(BF16)


def moved_rows(x_ref, lane, part):
    parts, ser, patches, _ = x_ref.shape
    lanes = QUAD * HEAD_DIM
    cube = x_ref[:, :, :, lane : lane + lanes].reshape(parts * ser, patches, lanes)
    return half_rows(cube, part)


def group_forward_body(
    scale, group_ref, x_ref, spread_ref, time_term_ref, prob_ref, term_ref, mixed, res
):
    parts, ser, patches, _ = x_ref.shape
    series = parts * ser
    width = mixed.shape[1]
    lanes = QUAD * HEAD_DIM
    half = patches // 2
    count = series * half
    row = lax.broadcasted_iota(jnp.int32, (count, 1), 0)
    column = lax.rem(lax.broadcasted_iota(jnp.int32, (1, QUAD * count), 1), count)
    id_key = group_ids(group_ref, row // half, lax.rem(row, half), series, half)
    id_query = group_ids(group_ref, column // half, lax.rem(column, half), series, half)
    keep = id_key == id_query
    for quad in range(width // lanes):
        start = lanes * quad
        for part in range(2):
            query = stacked(moved_rows(x_ref, start, part))
            key = moved_rows(x_ref, width + start, part)
            value = moved_rows(x_ref, 2 * width + start, part)
            prob = column_softmax(dot(key, query, NT), keep)
            prob_ref[quad, part] = prob
            out = unstacked(dot(prob.astype(BF16), value, TN))
            res[:, half * part : half * (part + 1), start : start + lanes] = out.reshape(
                series, half, lanes
            )
    mixed[...] = res[...].reshape(series * patches, width).astype(BF16)
    cot = x_ref[:, :, :, 3 * width :].reshape(series * patches, spread_ref.shape[1])
    term_ref[:, :width] = time_term_ref[...]
    term_ref[:, width:] = term_of(spread_ref, cot, mixed[...], scale)


def group_backward_body(place_ref, x_ref, prob_ref, mine_ref, other_ref, *rest):
    outs, (grad, weights, res) = rest[:-3], rest[-3:]
    parts, ser, patches, _ = x_ref.shape
    series = parts * ser
    width = grad.shape[1]
    lanes = QUAD * HEAD_DIM
    half = patches // 2
    cot = x_ref[:, :, :, 3 * width :].reshape(series * patches, weights.shape[1])
    back_project(cot, core_of(place_ref) == 1, mine_ref, other_ref, weights, grad)
    for quad in range(width // lanes):
        start = lanes * quad
        for part in range(2):
            query = stacked(moved_rows(x_ref, start, part))
            key = moved_rows(x_ref, width + start, part)
            value = moved_rows(x_ref, 2 * width + start, part)
            own_grad = grad[:, start : start + lanes].reshape(series, patches, lanes)
            grad_stack = stacked(half_rows(own_grad, part))
            gq, gk, gv = backward(prob_ref[quad, part], query, key, value, grad_stack)
            for index, result in enumerate((unstacked(gq), gk, gv)):
                spot = slice(width * index + start, width * index + start + lanes)
                res[:, half * part : half * (part + 1), spot] = result.reshape(series, half, lanes)
    for shift, out_ref in enumerate(outs):
        source = lax.rem(place_ref[0] + parts - shift, parts)
        out_ref[...] = res[pl.ds(ser * source, ser)].astype(BF16)


def first_sum_body(pad_ref, in_ref, out_ref):
    total = jnp.sum(in_ref[...].astype(F32), axis=0).astype(BF16)
    total = dot(pad_ref[...], total, NN)
    lows = total.shape[0] // 8
    width = total.shape[1] // 2
    for j in range(width // 128):
        chunks = [
            total[:, start : start + 128].reshape(lows, 8, 128)
            for start in (128 * j, width + 128 * j)
        ]
        out_ref[lows * j : lows * (j + 1)] = jnp.concatenate(chunks, axis=1).astype(BF16)


def last_sum_body(in_ref, time_ref, group_ref):
    total = jnp.sum(in_ref[...].astype(F32), axis=0)
    columns = time_ref.shape[0]
    time_ref[...] = total[:columns]
    group_ref[...] = total[8 : 8 + columns]


def tm_index(low, x, y, core):
    return ((low * X_SIZE + x) * Y_SIZE + y) * 2 + core


def first_groups():
    return [
        [tm_index(low, x, y, core) for x in range(X_SIZE) for core in range(2)]
        for low in range(LOW_SIZE)
        for y in range(Y_SIZE)
    ]


def along_x(shift):
    return [
        (tm_index(low, x, y, core), tm_index(low, (x + shift) % X_SIZE, y, core))
        for low in range(LOW_SIZE)
        for x in range(X_SIZE)
        for y in range(Y_SIZE)
        for core in range(2)
    ]


def second_groups(parts, count):
    return [
        [
            j * count + tm_index(low, x, y, core)
            for j in range(parts)
            for y in range(Y_SIZE)
            for low in range(LOW_SIZE)
        ]
        for x in range(X_SIZE)
        for core in range(2)
    ]


def spread_matrix(model, count):
    columns = model // count
    order = [
        columns * tm_index(low, x, y, core) + e
        for x in range(X_SIZE)
        for core in range(2)
        for y in range(Y_SIZE)
        for low in range(LOW_SIZE)
        for e in range(columns)
    ]
    return jnp.asarray(np.eye(model, dtype=np.float32)[order], BF16)


def pad_matrix(columns):
    lows = Y_SIZE * LOW_SIZE
    pad = np.zeros((lows, 8, lows, columns), np.float32)
    for low in range(lows):
        for e in range(columns):
            pad[low, e, low, e] = 1
    return jnp.asarray(pad.reshape(8 * lows, columns * lows), BF16)


def per_device(
    time_query,
    time_key,
    time_value,
    group_query,
    group_key,
    group_value,
    out_time,
    out_group,
    series_group,
    band_width,
    cotangent,
):
    ser, rows, width = time_query.shape
    model = cotangent.shape[2]
    parts = lax.axis_size("series")
    count = lax.axis_size("tm")
    columns = model // count
    scale = float(ser * parts * rows * count) ** (-0.5)
    place = lax.axis_index("tm")
    patches = rows // parts

    series = lax.axis_index("series")
    where = jnp.stack([series, place]).astype(jnp.int32)

    def over_series(value, shift):
        return lax.ppermute(value, "series", [(j, (j + shift) % parts) for j in range(parts)])

    sem = pltpu.SemaphoreType.DMA
    piece_rows = out_time.shape[0] // X_SIZE
    piece = call(
        piece_body,
        shape((parts, piece_rows, model), BF16),
        (where, out_time, out_group),
        0,
        500_000,
        smem=(0,),
    )
    column_piece = lax.all_to_all(piece, "series", 0, 0, tiled=True)
    rim = jnp.stack([time_key[:, rows - BAND :], time_value[:, rows - BAND :]])
    rim = lax.ppermute(rim, "tm", [(i, i + 1) for i in range(count - 1)])
    packed = call(
        pack_body,
        shape((parts, ser, patches, 3 * width + model), BF16),
        (group_query, group_key, group_value, cotangent),
        0,
        3_000_000,
    )
    packed, column_piece = lax.optimization_barrier((packed, column_piece))
    moved = lax.all_to_all(packed, "series", 0, 0, tiled=True)
    spread = spread_matrix(model, count)
    quads = width // (QUAD * HEAD_DIM)
    prob, term_time = call(
        functools.partial(time_forward_body, scale),
        (
            shape((ser, quads, rows + BAND, QUAD * rows), F32),
            shape((model, width), BF16),
        ),
        (where, band_width, time_query, time_key, time_value, rim, cotangent, spread),
        2_000_000_000,
        6_000_000,
        smem=(0, 1),
        scratch=[pltpu.VMEM((ser * rows, width), BF16)],
    )
    pieces = [column_piece] + [
        lax.ppermute(column_piece, "tm", along_x(shift)) for shift in range(1, X_SIZE)
    ]
    order, term_time = lax.optimization_barrier((where, term_time))
    weight_mine = call(
        gather_body,
        shape((X_SIZE, parts, piece_rows, model), BF16),
        (order, *pieces),
        0,
        1_600_000,
        smem=(0,),
        anywhere=True,
        scratch=[sem((X_SIZE,))],
        room=8192,
    )
    weight_other = lax.ppermute(weight_mine, "tm", [(i, i ^ 1) for i in range(count)])

    total = parts * ser * patches
    group_prob, term = call(
        functools.partial(group_forward_body, scale),
        (
            shape((quads, 2, total // 2, QUAD * total // 2), F32),
            shape((model, 2 * width), BF16),
        ),
        (series_group, moved, spread, term_time),
        4_000_000_000,
        8_000_000,
        smem=(0,),
        scratch=[
            pltpu.VMEM((total, width), BF16),
            pltpu.VMEM((parts * ser, patches, width), F32),
        ],
    )
    first = 2 * X_SIZE
    plane = lax.all_to_all(
        term.reshape(first, model // first, 2 * width),
        "tm",
        0,
        0,
        tiled=True,
        axis_index_groups=first_groups(),
    )
    back = call(
        group_backward_body,
        (shape((ser, patches, 3 * width), BF16),) * parts,
        (where, moved, group_prob, weight_mine, weight_other),
        40_000_000_000,
        8_000_000,
        smem=(0,),
        scratch=[
            pltpu.VMEM((total, width), BF16),
            pltpu.VMEM((width, model), BF16),
            pltpu.VMEM((parts * ser, patches, 3 * width), F32),
        ],
    )
    second = parts * Y_SIZE * LOW_SIZE
    chunks = call(
        first_sum_body,
        shape((second, 16, 128), BF16),
        (pad_matrix(columns), plane),
        0,
        500_000,
        room=8192,
    )
    returned = [back[0]] + [over_series(back[shift], -shift) for shift in range(1, parts)]

    chunks, order, _ = lax.optimization_barrier((chunks, where, back[0]))
    grad_tq, grad_tk, grad_tv, tail, rim_grad = call(
        time_backward_body,
        (
            shape((ser, rows, width), BF16),
            shape((ser, rows, width), BF16),
            shape((ser, rows, width), BF16),
            shape((2, ser, BAND, width), F32),
            shape((2, ser, BAND, width), BF16),
        ),
        (
            order,
            prob,
            time_query,
            time_key,
            time_value,
            rim,
            cotangent,
            weight_mine,
            weight_other,
        ),
        40_000_000_000,
        6_000_000,
        smem=(0,),
        scratch=[pltpu.VMEM((ser * rows, width), BF16), pltpu.VMEM((width, model), BF16)],
    )
    rim_back = lax.ppermute(rim_grad, "tm", [(i + 1, i) for i in range(count - 1)])
    grad_gq, grad_gk, grad_gv = call(
        unpack_body,
        (shape((ser, rows, width), BF16),) * 3,
        (where, *returned),
        0,
        2_000_000,
        smem=(0,),
        anywhere=True,
        scratch=[sem((3 * parts,))],
        room=8192,
    )
    rim_back, grad_gq = lax.optimization_barrier((rim_back, grad_gq))
    border = pl.BlockSpec((ser, BAND, width), lambda i: (0, rows // BAND - 1, 0))
    grad_tk, grad_tv = pl.pallas_call(
        time_join_body,
        out_shape=(shape((ser, rows, width), BF16),) * 2,
        grid=(1,),
        in_specs=[pl.BlockSpec(memory_space=pl.ANY)] * 2 + [block(tail, ""), block(rim_back, "")],
        out_specs=[border] * 2,
        input_output_aliases={0: 0, 1: 1},
        compiler_params=pltpu.CompilerParams(vmem_limit_bytes=60 * 1024 * 1024),
        cost_estimate=pl.CostEstimate(flops=0, bytes_accessed=1_000_000, transcendentals=0),
    )(grad_tk, grad_tv, tail, rim_back)
    chunks = lax.all_to_all(
        chunks,
        ("series", "tm"),
        0,
        0,
        tiled=True,
        axis_index_groups=second_groups(parts, count),
    )
    grad_wt, grad_wg = call(
        last_sum_body, (shape((columns, 128), F32),) * 2, (chunks,), 0, 100_000, room=8192
    )
    return (grad_tq, grad_tk, grad_tv, grad_gq, grad_gk, grad_gv, grad_wt.T, grad_wg.T)


def solution(mesh):
    rows = P("series", "tm", None)
    return jax.shard_map(
        per_device,
        mesh=mesh,
        in_specs=(rows,) * 6 + (P("series", None),) * 2 + (P(), P(), rows),
        out_specs=(rows,) * 6 + (P("series", "tm"),) * 2,
        check_vma=False,
    )
```
